128 devices in a mesh: grp: 8 (over y, core), sub: 16 (over x, z).
Axes of the slice: x: 4, y: 4, z: 4, core: 2. Of those that a mesh axis runs over, the one named last changes fastest.
Arguments:
- embeddings: bfloat16 [49152, 1024], P(('grp', 'sub')), may hold values from -6 to 6
- cluster_ids: int32 [49152], P(('grp', 'sub')), may hold values from 0 to 23, as said below
Outputs:
- best_similarity: float32 [49152], P(('grp', 'sub'))
The draws below stay inside these ranges and needn't reach their ends.
Inputs may be any that keep to these rules, and one draw needn't show every extreme that they name: `cluster_ids`: cluster c belongs to group c // 3. Of the 384 embeddings of each device, exactly 96 lie in the clusters of one group, and the others are spread as evenly as possible over the other groups; which group is the one with 96 depends only on the device's index along sub.
All inputs are finite; a program needn't handle non-finite values.
Results may differ from the reference program's by a relative error of at most 0.0003.
Values may be sent and summed in bfloat16 or wider, within the bound.
No kernel may reach another device: no remote copies, remote signals or barrier semaphores. Data moves between devices by JAX's collectives and lax.ppermute only.
A program may use at most 128 MiB of HBM per device.

```python
import jax
import jax.numpy as jnp
from jax import lax

D = 1024
ROWS_DEV = 384
KG = 3
CAP = 96
ROWS = 49152
N_GRP = 8
N_SUB = 16


def draw_cluster_ids(key, part):
    key = jax.random.fold_in(key, 7)
    key_offset, key_shuffle, key_first, key_second = jax.random.split(key, 4)
    groups_count = N_GRP
    device_count = N_GRP * N_SUB
    device_index = jnp.arange(device_count, dtype=jnp.int32)
    sub_index = device_index % N_SUB
    offset = jax.random.randint(key_offset, (), 0, groups_count, dtype=jnp.int32)
    heavy_group = (sub_index + offset) % groups_count
    row_index = jnp.arange(ROWS_DEV, dtype=jnp.int32)
    other_group = (heavy_group[:, None] + 1 + (row_index[None, :] - CAP) % (groups_count - 1)) % groups_count
    group_table = jnp.where(row_index[None, :] < CAP, heavy_group[:, None], other_group)
    shuffle_keys = jax.random.split(key_shuffle, device_count)
    shuffles = jax.vmap(lambda single: jax.random.permutation(single, ROWS_DEV))(shuffle_keys)
    group_table = jnp.take_along_axis(group_table, shuffles.astype(jnp.int32), axis=1)
    first_pick = jax.random.randint(key_first, (device_count, ROWS_DEV), 0, KG, dtype=jnp.int32)
    second_pick = jax.random.randint(key_second, (device_count, ROWS_DEV), 0, KG, dtype=jnp.int32)
    local_index = jnp.minimum(first_pick, second_pick)
    cluster_index = group_table * KG + local_index
    return cluster_index.reshape(ROWS).astype(jnp.int32)


def levels(key, extent, cuts, low, high):
    factor_of = 1.0
    for dim, parts in cuts:
        draws = jax.random.uniform(jax.random.fold_in(jax.random.fold_in(key, 6), dim), (parts,), jnp.float32, low / len(cuts), high / len(cuts))
        factor_of = factor_of * jnp.repeat(jnp.exp(draws), extent[dim] // parts).reshape((-1,) + (1,) * (len(extent) - 1 - dim))
    return factor_of


def scatter_about(rng, shape, spread, limit, shards=(), kind=jnp.bfloat16):
    entries = jax.random.normal(rng, shape, jnp.float32) * spread
    if len(shards) > 0:
        entries = levels(rng, shape, shards, -0.22, 0.18) * entries
    return jnp.clip(entries, min=-limit, max=limit).astype(kind)


def setup_inputs(seed: int = 0) -> dict:
    seeds = jax.random.split(jax.random.key(seed), 3)
    return {
        "embeddings": scatter_about(seeds[0], (ROWS, D), 1.0, 6.0, ((0, 128),)),
        "cluster_ids": draw_cluster_ids(jax.random.fold_in(seeds[2], 71), 0),
    }


EPSILON = 1e-06

def reference(embeddings, cluster_ids):
    as_float = embeddings.astype(jnp.float32)
    inverse = lax.rsqrt(lax.optimization_barrier(jnp.sum(as_float * as_float, axis=1)) + EPSILON)
    total_rows = as_float.shape[0]
    block_rows = 512 if total_rows % 512 == 0 else total_rows
    block_count = total_rows // block_rows
    positions = jnp.arange(total_rows, dtype=jnp.int32)

    def one_block(index):
        first_row = (index * block_rows).astype(jnp.int32)
        left_rows = lax.dynamic_slice_in_dim(as_float, first_row, block_rows, 0)
        left_inverse = lax.dynamic_slice_in_dim(inverse, first_row, block_rows, 0)
        left_ids = lax.dynamic_slice_in_dim(cluster_ids, first_row, block_rows, 0)
        left_index = lax.dynamic_slice_in_dim(positions, first_row, block_rows, 0)
        scores = jnp.dot(left_rows, as_float.T, precision=lax.Precision.HIGHEST)
        scaled = scores * left_inverse[:, None] * inverse[None, :]
        same_cluster = (left_ids[:, None] == cluster_ids[None, :]) & (left_index[:, None] != positions[None, :])
        masked = jnp.where(same_cluster, scaled, jnp.float32(-1.0))
        return lax.optimization_barrier(jnp.max(masked, axis=1))
    result = lax.map(one_block, jnp.arange(block_count, dtype=jnp.int32))
    return result.reshape(total_rows)
```

```python
import functools
import math

import jax
import jax.numpy as jnp
from jax import lax
from jax.experimental import pallas as pl
from jax.experimental.pallas import tpu as pltpu
from jax.sharding import PartitionSpec as P

KG = 3
CAP = 96
EPSILON = 1e-06

ROWS = 384
CHUNK = 48
LIGHT = 42
EXTRA = 64
FIRST = 4 * CHUNK
SECOND = 4 * CHUNK + EXTRA
PARTS = (FIRST, SECOND)
LANES = 512
LOW = -1e30

STEPS = ((1, 1), (0, 1), (1, 3), (0, 3), (1, 2), (1, 0), (0, 2))

VMEM = pl.BlockSpec(memory_space=pltpu.VMEM)
PARAMS = pltpu.CompilerParams(vmem_limit_bytes=48 * 1024 * 1024)


def inverse_norms(block):
    values = block.astype(jnp.float32)
    return lax.rsqrt(jnp.sum(values * values, axis=1) + EPSILON)


def tile_max(left_rows, left_ids, left_inverse, right_rows, right_ids, right_inverse, left_first, right_first):
    scores = lax.dot_general(
        left_rows, right_rows, (((1,), (1,)), ((), ())), preferred_element_type=jnp.float32
    )
    scaled = scores * left_inverse[:, None] * right_inverse[None, :]
    left_index = left_first + jnp.arange(left_rows.shape[0], dtype=jnp.int32)
    right_index = right_first + jnp.arange(right_rows.shape[0], dtype=jnp.int32)
    same_cluster = (
        (left_ids[:, None] == right_ids[None, :])
        & (left_ids[:, None] >= 0)
        & (left_index[:, None] != right_index[None, :])
    )
    masked = jnp.where(same_cluster, scaled, jnp.float32(-1.0))
    return jnp.max(masked, axis=1)


def general(embeddings, cluster_ids):
    groups_count = lax.axis_size("grp")
    feature_count = embeddings.shape[1]
    destination = cluster_ids // KG
    onehot = (destination[:, None] == jnp.arange(groups_count, dtype=jnp.int32)[None, :]).astype(jnp.int32)
    earlier = jnp.cumsum(onehot, axis=0) - onehot
    slot_index = jnp.sum(earlier * onehot, axis=1)
    position = destination * CAP + slot_index
    send_rows = jnp.zeros((groups_count * CAP, feature_count), jnp.bfloat16).at[position].set(embeddings)
    send_ids = (
        jnp.full((groups_count * CAP,), -1.0, jnp.bfloat16).at[position].set(cluster_ids.astype(jnp.bfloat16))
    )
    own_rows = lax.all_to_all(send_rows, "grp", split_axis=0, concat_axis=0, tiled=True)
    own_ids = lax.all_to_all(send_ids, "grp", split_axis=0, concat_axis=0, tiled=True)
    own_count = own_rows.shape[0]
    own_inverse = inverse_norms(own_rows)
    sub_count = lax.axis_size("sub")
    own_sub = lax.axis_index("sub")
    ring = [(index, (index + 1) % sub_count) for index in range(sub_count)]

    def one_block(index, state):
        right_rows, right_ids, current = state
        row_max = tile_max(
            own_rows,
            own_ids,
            own_inverse,
            right_rows,
            right_ids,
            inverse_norms(right_rows),
            own_sub * own_count,
            ((own_sub - index) % sub_count) * own_count,
        )
        next_rows = lax.ppermute(right_rows, "sub", ring)
        next_ids = lax.ppermute(right_ids, "sub", ring)
        return next_rows, next_ids, jnp.maximum(current, row_max)

    start = (own_rows, own_ids, jnp.full((own_count,), -1.0, jnp.float32))
    best_seen = lax.fori_loop(0, sub_count, one_block, start)[2]
    gathered_back = lax.all_to_all(best_seen, "grp", split_axis=0, concat_axis=0, tiled=True)
    return jnp.take(gathered_back, position, axis=0)


def iota(shape, dim):
    return lax.broadcasted_iota(jnp.int32, shape, dim)


def dot_nt(left, right):
    return lax.dot_general(left, right, (((1,), (1,)), ((), ())), preferred_element_type=jnp.float32)


def dot_nn(left, right):
    return lax.dot_general(left, right, (((1,), (0,)), ((), ())), preferred_element_type=jnp.float32)


def three_parts(value):
    high = value.astype(jnp.bfloat16).astype(jnp.float32)
    rest = value - high
    middle = rest.astype(jnp.bfloat16).astype(jnp.float32)
    low = (rest - middle).astype(jnp.bfloat16).astype(jnp.float32)
    return high, middle, low


def as_bf16(mask):
    return jnp.where(mask, 1.0, 0.0).astype(jnp.bfloat16)


def owner_at(place_ref, step):
    dx, dz = (0, 0) if step < 0 else STEPS[step]
    return ((place_ref[0] + dx) % 2) * 4 + (place_ref[1] + dz) % 4


def lane_of_slot(slot):
    return slot * CHUNK if slot < 4 else 256 + (slot - 4) * CHUNK


def sort_kernel(at_ref, ids_ref, rows_ref, *out_refs):
    chunk_refs, extra_ref, lane_ref, home_ref = out_refs[:8], out_refs[8], out_refs[9], out_refs[10]
    ids = ids_ref[...].reshape(1, ROWS)
    group_of = iota((8, ROWS), 0)
    member = (ids >= group_of * KG) & (ids < group_of * KG + KG)
    member_f = jnp.where(member, 1.0, 0.0)
    before = as_bf16(iota((ROWS, ROWS), 0) < iota((ROWS, ROWS), 1))
    ranks = dot_nn(member_f.astype(jnp.bfloat16), before)
    rank = jnp.sum(member_f * ranks, axis=0, keepdims=True)
    group = jnp.sum(member_f * group_of.astype(jnp.float32), axis=0, keepdims=True)
    count = jnp.sum(member_f, axis=1, keepdims=True)
    most = jnp.where(count > 64.0, 1.0, 0.0)
    home = jnp.sum(most * iota((8, 1), 0).astype(jnp.float32), axis=0, keepdims=True)
    home_ref[...] = jnp.broadcast_to(home, home_ref.shape)
    values = rows_ref[...].astype(jnp.float32)
    inverse_column = lax.rsqrt(jnp.sum(values * values, axis=1, keepdims=True) + EPSILON)
    diagonal = iota((ROWS, ROWS), 0) == iota((ROWS, ROWS), 1)
    inverse = jnp.sum(jnp.where(diagonal, inverse_column, 0.0), axis=0, keepdims=True)
    high, middle, low = three_parts(inverse)
    line = iota((16, ROWS), 0)
    told = jnp.where(line == 10, ids.astype(jnp.float32) + 1.0, 0.0)
    told = jnp.where(line == 11, high, told)
    told = jnp.where(line == 12, middle, told)
    told = jnp.where(line == 13, low, told)
    lane = jnp.full((1, ROWS), -1.0, jnp.float32)
    tolds = []
    for slot in range(8):
        goes = (group == owner_at(at_ref, slot - 1).astype(jnp.float32)) & (rank < float(LIGHT))
        lane = jnp.where(goes, rank + float(lane_of_slot(slot)), lane)
        tolds.append(jnp.where(goes, told, 0.0))
    goes = (group == home) & (rank >= float(LIGHT))
    lane = jnp.where(goes, rank + float(lane_of_slot(8) - LIGHT), lane)
    tolds.append(jnp.where(goes, told, 0.0))
    lane_ref[...] = jnp.broadcast_to(lane, lane_ref.shape)
    pick = as_bf16(iota((LANES, ROWS), 0) == lane.astype(jnp.int32))
    data = dot_nn(pick, rows_ref[...])
    placed = dot_nt(jnp.concatenate(tolds, axis=0).astype(jnp.bfloat16), pick)
    for slot in range(9):
        ref = chunk_refs[slot] if slot < 8 else extra_ref
        first, count = lane_of_slot(slot), CHUNK if slot < 8 else EXTRA
        part = 0 if slot < 4 else 256
        ref[0 : count - 16, :] = data[first : first + count - 16].astype(jnp.bfloat16)
        tail = data[first + count - 16 : first + count]
        if slot == 8:
            tail = jnp.where(iota(tail.shape, 0) == 15, home + 1.0, tail)
        ref[count - 16 : count, :] = tail.astype(jnp.bfloat16)
        ref[count - 16 : count, 0:256] = (
            tail[:, 0:256] + placed[16 * slot : 16 * slot + 16, part : part + 256]
        ).astype(jnp.bfloat16)


def marked(ref):
    return ref[EXTRA - 16 : EXTRA, :].astype(jnp.float32)[15:16, 0:1]


def half_kernel(at_ref, own_ref, other_ref, out_ref):
    parity = at_ref[0] % 2
    own_fits = jnp.where(marked(own_ref) >= 5.0, 1, 0) == parity
    other_fits = jnp.where(marked(other_ref) >= 5.0, 1, 0) == parity
    taken = jnp.where(own_fits, own_ref[...], other_ref[...])
    out_ref[0 : EXTRA - 16, :] = taken[0 : EXTRA - 16]
    tail = taken[EXTRA - 16 : EXTRA].astype(jnp.float32)
    clash = (iota(tail.shape, 0) == 15) & (own_fits == other_fits)
    out_ref[EXTRA - 16 : EXTRA, :] = jnp.where(clash, 0.0, tail).astype(jnp.bfloat16)


def block_kernel(at_ref, *refs):
    chunks, extras, out_ref = refs[0:4], refs[4:8], refs[8]
    wanted = owner_at(at_ref, -1).astype(jnp.float32) + 1.0
    for index in range(4):
        out_ref[index * CHUNK : (index + 1) * CHUNK, :] = chunks[index][...]
    found = jnp.zeros((1, 1), jnp.float32)
    held = jnp.ones((1, 1), jnp.float32)
    taken = extras[0][...]
    for index in range(4):
        mark = marked(extras[index])
        found = found + jnp.where(mark == wanted, 1.0, 0.0)
        held = jnp.where(mark == 0.0, 0.0, held)
        if index > 0:
            taken = jnp.where(mark == wanted, extras[index][...], taken)
    good = jnp.where((found == 1.0) & (held == 1.0), 1.0, 0.0)
    out_ref[4 * CHUNK : SECOND - 16, :] = taken[0 : EXTRA - 16]
    tail = taken[EXTRA - 16 : EXTRA].astype(jnp.float32)
    out_ref[SECOND - 16 : SECOND, :] = jnp.where(iota(tail.shape, 0) == 14, good, tail).astype(jnp.bfloat16)


def told_of(ref, part):
    total = jnp.zeros((16, 256), jnp.float32)
    ends = [CHUNK, 2 * CHUNK, 3 * CHUNK, 4 * CHUNK] + ([SECOND] if part else [])
    for end in ends:
        total = total + ref[end - 16 : end, 0:256].astype(jnp.float32)
    rows = PARTS[part]
    return total[10:11, 0:rows], (total[11:12] + total[12:13] + total[13:14])[:, 0:rows], total[14:15, 0:1]


def column_of(row):
    count = row.shape[1]
    diagonal = iota((count, count), 0) == iota((count, count), 1)
    return jnp.sum(jnp.where(diagonal, row, 0.0), axis=1, keepdims=True)


def best_of(lefts, rights, own, out_refs):
    left_known = [[told_of(ref, part) for part, ref in enumerate(left)] for left in lefts]
    best = [[jnp.full((1, rows), LOW, jnp.float32) for rows in PARTS] for _ in lefts]
    for right_index, right in enumerate(rights):
        for right_part, right_ref in enumerate(right):
            ids, inverse, _ = told_of(right_ref, right_part)
            ids, inverse = column_of(ids), column_of(inverse)
            rows = right_ref[...]
            for left_index, left in enumerate(lefts):
                for left_part, left_ref in enumerate(left):
                    scores = dot_nt(rows, left_ref[...]) * inverse
                    alike = ids == left_known[left_index][left_part][0]
                    if own and left_index == 0 and right_index == 0 and left_part == right_part:
                        alike = alike & (iota(scores.shape, 0) != iota(scores.shape, 1))
                    top = jnp.max(jnp.where(alike, scores, LOW), axis=0, keepdims=True)
                    best[left_index][left_part] = jnp.maximum(best[left_index][left_part], top)
    for left_index, out_ref in enumerate(out_refs):
        out_ref[...] = jnp.full(out_ref.shape, -1.0, jnp.float32)
        for part, rows in enumerate(PARTS):
            inverse = left_known[left_index][part][1]
            out_ref[0:1, 256 * part : 256 * part + rows] = jnp.maximum(best[left_index][part] * inverse, -1.0)


def match_kernel(left_count, right_count, own, checked, *refs):
    pairs = [(refs[2 * index], refs[2 * index + 1]) for index in range(left_count + right_count)]
    out_refs = refs[2 * (left_count + right_count) :]
    best_of(pairs[:left_count], pairs[left_count:], own, out_refs)
    if checked:
        good = jnp.minimum(told_of(pairs[0][1], 1)[2], told_of(pairs[left_count][1], 1)[2])
        out_refs[0][1:2, :] = jnp.broadcast_to(good, (1, LANES))


def far_kernel(first_a, first_b, second_a, second_b, *refs):
    rights = [(refs[2 * index], refs[2 * index + 1]) for index in range(4)]
    out_ref, first, second = refs[8], refs[9], refs[10]
    first[0 : FIRST // 2, :] = first_a[...]
    first[FIRST // 2 : FIRST, :] = first_b[...]
    second[0 : SECOND // 2, :] = second_a[...]
    second[SECOND // 2 : SECOND, :] = second_b[...]
    best_of([(first, second)], rights, False, [out_ref])


def final_kernel(at_ref, own_ref, side_ref, z1_ref, z2_ref, z3_ref, lane_ref, home_ref, out_ref, ok_ref):
    lane = iota((1, LANES), 1)
    own = own_ref[0:1, :]
    good = own_ref[1:2, :]
    home = home_ref[0:1, 0:1]
    extra = jnp.where(home == owner_at(at_ref, -1).astype(jnp.float32), own, -1.0)
    total = own
    sources = {1: z1_ref, 2: z2_ref, 3: z3_ref}
    for step, (dx, dz) in enumerate(STEPS):
        ref, row = (side_ref, 0) if dz == 0 else (sources[dz], 8 * dx)
        vector = ref[row : row + 1, :]
        good = jnp.minimum(good, ref[row + 1 : row + 2, :])
        first = lane_of_slot(step + 1)
        total = jnp.where((lane >= first) & (lane < first + CHUNK), vector, total)
        extra = jnp.where(home == owner_at(at_ref, step).astype(jnp.float32), vector, extra)
    total = jnp.where(lane >= lane_of_slot(8), extra, total)
    high, middle, low = three_parts(total)
    line = iota((16, LANES), 0)
    parts = jnp.where(line == 0, high, jnp.where(line == 1, middle, jnp.where(line == 2, low, 0.0)))
    pick = as_bf16(iota((LANES, ROWS), 0) == lane_ref[0:1, :].astype(jnp.int32))
    picked = dot_nn(parts.astype(jnp.bfloat16), pick)
    out_ref[...] = jnp.sum(picked, axis=0, keepdims=True).reshape(ROWS)
    ok_ref[...] = jnp.where(good[:, 0:128] == 1.0, 1, 0)


SMEM = pl.BlockSpec(memory_space=pltpu.SMEM)


def call(kernel, outs, *args, scalars=0, scratch=(), flops=0):
    read = sum(math.prod(a.shape) * a.dtype.itemsize for a in args)
    return pl.pallas_call(
        kernel,
        out_shape=outs,
        in_specs=[SMEM] * scalars + [VMEM] * (len(args) - scalars),
        out_specs=[VMEM] * len(outs) if isinstance(outs, list) else VMEM,
        scratch_shapes=list(scratch),
        compiler_params=PARAMS,
        cost_estimate=pl.CostEstimate(flops=flops, bytes_accessed=read, transcendentals=0),
    )(*args)


def along_sub(value, to_x, to_z):
    perm = [(4 * x + z, 4 * to_x(x) + to_z(z)) for x in range(4) for z in range(4)]
    return lax.ppermute(value, "sub", perm)


def along_grp(value, to_y, to_core):
    perm = [(2 * y + c, 2 * to_y(y) + to_core(c)) for y in range(4) for c in range(2)]
    return lax.ppermute(value, "grp", perm)


def same(index):
    return index


def shift(amount):
    return lambda index: (index + amount) % 4


def flip(amount):
    return lambda index: index ^ amount


def local(embeddings, cluster_ids):
    f32, bf16 = jnp.float32, jnp.bfloat16
    width = embeddings.shape[1]
    shape = jax.ShapeDtypeStruct
    sub = lax.axis_index("sub")
    at = jnp.stack([sub // 4, sub % 4]).astype(jnp.int32)
    *chunks, extra, lane, home = call(
        sort_kernel,
        [shape((CHUNK, width), bf16)] * 8
        + [shape((EXTRA, width), bf16), shape((8, ROWS), f32), shape((8, 128), f32)],
        at,
        cluster_ids,
        embeddings,
        scalars=1,
        flops=500_000_000,
    )
    other_extra = along_sub(extra, flip(1), same)
    got = [chunks[0]] + [along_sub(chunk, flip(dx), shift(dz)) for chunk, (dx, dz) in zip(chunks[1:], STEPS)]
    extra = call(half_kernel, shape((EXTRA, width), bf16), at, extra, other_extra, scalars=1)
    extras = [extra] + [along_sub(extra, same, shift(dz)) for dz in (1, 2, 3)]
    first = jnp.concatenate(got[:4], axis=0)
    second = call(block_kernel, shape((SECOND, width), bf16), at, *got[4:], *extras, scalars=1)
    block = (first, second)
    below = tuple(along_grp(part, shift(1), same) for part in block)
    above = tuple(along_grp(part, shift(-1), same) for part in block)
    across = tuple(along_sub(part, shift(2), same) for part in block)
    sibling = tuple(along_grp(part, same, flip(1)) for part in block)
    across_sibling = tuple(along_grp(part, same, flip(1)) for part in across)
    far = [along_grp(part[: part.shape[0] // 2], shift(1), same) for part in below]
    far += [along_grp(part[part.shape[0] // 2 :], shift(-1), same) for part in above]
    flops = 2 * sum(PARTS) ** 2 * width
    vector = shape((8, LANES), f32)
    near = (*block, *sibling)
    others = (*across, *across_sibling)

    def match(lefts, rights, own=False, checked=False):
        kernel = functools.partial(match_kernel, len(lefts) // 2, len(rights) // 2, own, checked)
        work = flops * len(lefts) * len(rights) // 4
        out = call(kernel, [vector] * (len(lefts) // 2), *lefts, *rights, flops=work)
        return out

    (best_near,) = match(block, near, own=True)
    below_near, above_near = match((*below, *above), near)
    best, below_other, above_other = match((*block, *below, *above), others, checked=True)
    from_above = along_grp(jnp.maximum(below_near, below_other), shift(-1), same)
    from_below = along_grp(jnp.maximum(above_near, above_other), shift(1), same)
    best_far = call(
        far_kernel,
        vector,
        far[0],
        far[2],
        far[1],
        far[3],
        *near,
        *others,
        scratch=[pltpu.VMEM((rows, width), bf16) for rows in PARTS],
        flops=4 * flops,
    )
    from_far = along_grp(best_far, shift(2), same)
    best = jnp.maximum(jnp.maximum(best, best_near), jnp.maximum(from_above, from_below))
    best = jnp.maximum(best, from_far)
    side = along_sub(best, flip(1), same)
    both = jnp.concatenate([best, side], axis=0)
    pulled = [along_sub(both, same, shift(-dz)) for dz in (1, 2, 3)]
    out, ok = call(
        final_kernel,
        [shape((ROWS,), f32), shape((1, 128), jnp.int32)],
        at,
        best,
        side,
        *pulled,
        lane,
        home,
        scalars=1,
    )
    return lax.cond(ok[0, 0] == 1, lambda e, c, o: o, lambda e, c, o: general(e, c), embeddings, cluster_ids, out)


def solution(mesh):
    return jax.shard_map(
        local,
        mesh=mesh,
        in_specs=(P(("grp", "sub"), None), P(("grp", "sub"))),
        out_specs=P(("grp", "sub")),
        check_vma=False,
    )
```

```python
import functools
import math

import jax
import jax.numpy as jnp
from jax import lax
from jax.experimental import pallas as pl
from jax.experimental.pallas import tpu as pltpu
from jax.sharding import PartitionSpec as P

KG = 3
CAP = 96
EPSILON = 1e-06

ROWS = 384
OWNERS = 8
CHUNK = 48
LIGHT = 42
MAIN = OWNERS * CHUNK
EXTRA = 64
BLOCK = MAIN + EXTRA
LANES = 512
LOW = -1e30

STEPS = ((1, 0), (0, 1), (0, 3), (1, 1), (1, 3), (1, 2), (0, 2))

VMEM = pl.BlockSpec(memory_space=pltpu.VMEM)
PARAMS = pltpu.CompilerParams(vmem_limit_bytes=48 * 1024 * 1024)


def inverse_norms(block):
    values = block.astype(jnp.float32)
    return lax.rsqrt(jnp.sum(values * values, axis=1) + EPSILON)


def tile_max(left_rows, left_ids, left_inverse, right_rows, right_ids, right_inverse, left_first, right_first):
    scores = lax.dot_general(
        left_rows, right_rows, (((1,), (1,)), ((), ())), preferred_element_type=jnp.float32
    )
    scaled = scores * left_inverse[:, None] * right_inverse[None, :]
    left_index = left_first + jnp.arange(left_rows.shape[0], dtype=jnp.int32)
    right_index = right_first + jnp.arange(right_rows.shape[0], dtype=jnp.int32)
    same_cluster = (
        (left_ids[:, None] == right_ids[None, :])
        & (left_ids[:, None] >= 0)
        & (left_index[:, None] != right_index[None, :])
    )
    masked = jnp.where(same_cluster, scaled, jnp.float32(-1.0))
    return jnp.max(masked, axis=1)


def general(embeddings, cluster_ids):
    groups_count = lax.axis_size("grp")
    feature_count = embeddings.shape[1]
    destination = cluster_ids // KG
    onehot = (destination[:, None] == jnp.arange(groups_count, dtype=jnp.int32)[None, :]).astype(jnp.int32)
    earlier = jnp.cumsum(onehot, axis=0) - onehot
    slot_index = jnp.sum(earlier * onehot, axis=1)
    position = destination * CAP + slot_index
    send_rows = jnp.zeros((groups_count * CAP, feature_count), jnp.bfloat16).at[position].set(embeddings)
    send_ids = (
        jnp.full((groups_count * CAP,), -1.0, jnp.bfloat16).at[position].set(cluster_ids.astype(jnp.bfloat16))
    )
    own_rows = lax.all_to_all(send_rows, "grp", split_axis=0, concat_axis=0, tiled=True)
    own_ids = lax.all_to_all(send_ids, "grp", split_axis=0, concat_axis=0, tiled=True)
    own_count = own_rows.shape[0]
    own_inverse = inverse_norms(own_rows)
    sub_count = lax.axis_size("sub")
    own_sub = lax.axis_index("sub")
    ring = [(index, (index + 1) % sub_count) for index in range(sub_count)]

    def one_block(index, state):
        right_rows, right_ids, current = state
        row_max = tile_max(
            own_rows,
            own_ids,
            own_inverse,
            right_rows,
            right_ids,
            inverse_norms(right_rows),
            own_sub * own_count,
            ((own_sub - index) % sub_count) * own_count,
        )
        next_rows = lax.ppermute(right_rows, "sub", ring)
        next_ids = lax.ppermute(right_ids, "sub", ring)
        return next_rows, next_ids, jnp.maximum(current, row_max)

    start = (own_rows, own_ids, jnp.full((own_count,), -1.0, jnp.float32))
    best_seen = lax.fori_loop(0, sub_count, one_block, start)[2]
    gathered_back = lax.all_to_all(best_seen, "grp", split_axis=0, concat_axis=0, tiled=True)
    return jnp.take(gathered_back, position, axis=0)


def iota(shape, dim):
    return lax.broadcasted_iota(jnp.int32, shape, dim)


def dot_nt(left, right):
    return lax.dot_general(left, right, (((1,), (1,)), ((), ())), preferred_element_type=jnp.float32)


def dot_nn(left, right):
    return lax.dot_general(left, right, (((1,), (0,)), ((), ())), preferred_element_type=jnp.float32)


def three_parts(value):
    high = value.astype(jnp.bfloat16).astype(jnp.float32)
    rest = value - high
    middle = rest.astype(jnp.bfloat16).astype(jnp.float32)
    low = (rest - middle).astype(jnp.bfloat16).astype(jnp.float32)
    return high, middle, low


def as_bf16(mask):
    return jnp.where(mask, 1.0, 0.0).astype(jnp.bfloat16)


def owner_at(place_ref, dx, dz):
    return ((place_ref[0] + dx) % 2) * 4 + (place_ref[1] + dz) % 4


def sort_kernel(at_ref, ids_ref, rows_ref, *out_refs):
    chunk_refs, extra_ref, known_ref = out_refs[:OWNERS], out_refs[OWNERS], out_refs[OWNERS + 1]
    ids = ids_ref[...].reshape(1, ROWS)
    group_of = iota((OWNERS, ROWS), 0)
    member = (ids >= group_of * KG) & (ids < group_of * KG + KG)
    member_f = jnp.where(member, 1.0, 0.0)
    before = as_bf16(iota((ROWS, ROWS), 0) < iota((ROWS, ROWS), 1))
    ranks = dot_nn(member_f.astype(jnp.bfloat16), before)
    rank = jnp.sum(member_f * ranks, axis=0, keepdims=True)
    group = jnp.sum(member_f * group_of.astype(jnp.float32), axis=0, keepdims=True)
    count = jnp.sum(member_f, axis=1, keepdims=True)
    most = jnp.where(count > 64.0, 1.0, 0.0)
    home = jnp.sum(most * iota((OWNERS, 1), 0).astype(jnp.float32), axis=0, keepdims=True)
    values = rows_ref[...].astype(jnp.float32)
    inverse_column = lax.rsqrt(jnp.sum(values * values, axis=1, keepdims=True) + EPSILON)
    diagonal = iota((ROWS, ROWS), 0) == iota((ROWS, ROWS), 1)
    inverse = jnp.sum(jnp.where(diagonal, inverse_column, 0.0), axis=0, keepdims=True)
    high, middle, low = three_parts(inverse)
    line = iota((16, ROWS), 0)
    told = jnp.where(line == 10, ids.astype(jnp.float32) + 1.0, 0.0)
    told = jnp.where(line == 11, high, told)
    told = jnp.where(line == 12, middle, told)
    told = jnp.where(line == 13, low, told)
    rest = (group == home) & (rank >= float(LIGHT))
    lane = jnp.where(rest, rank + float(MAIN - LIGHT), -1.0)
    tolds = []
    for slot, (dx, dz) in enumerate(((0, 0), *STEPS)):
        goes = (group == owner_at(at_ref, dx, dz).astype(jnp.float32)) & (rank < float(LIGHT))
        lane = jnp.where(goes, rank + float(slot * CHUNK), lane)
        tolds.append(jnp.where(goes, told, 0.0))
    tolds.append(jnp.where(rest, told, 0.0))
    known_ref[...] = jnp.where(line == 0, lane, group)[0:8]
    pick = as_bf16(iota((LANES, ROWS), 0) == lane.astype(jnp.int32))
    data = dot_nn(pick, rows_ref[...])
    placed = dot_nt(jnp.concatenate(tolds, axis=0).astype(jnp.bfloat16), pick)
    for slot, ref in enumerate(chunk_refs):
        first = slot * CHUNK
        ref[0:32, :] = data[first : first + 32].astype(jnp.bfloat16)
        tail = data[first + 32 : first + CHUNK]
        ref[32:CHUNK, :] = tail.astype(jnp.bfloat16)
        ref[32:CHUNK, 0:MAIN] = (tail[:, 0:MAIN] + placed[16 * slot : 16 * slot + 16, 0:MAIN]).astype(jnp.bfloat16)
    extra_ref[0:48, :] = data[MAIN : MAIN + 48].astype(jnp.bfloat16)
    tail = data[MAIN + 48 : BLOCK]
    tail = jnp.where(iota(tail.shape, 0) == 15, home + 1.0, tail)
    extra_ref[48:EXTRA, :] = tail.astype(jnp.bfloat16)
    extra_ref[48:EXTRA, 0:128] = (
        tail[:, 0:128] + placed[16 * OWNERS : 16 * OWNERS + 16, MAIN:LANES]
    ).astype(jnp.bfloat16)


def marked(ref):
    return ref[EXTRA - 16 : EXTRA, :].astype(jnp.float32)[15:16, 0:1]


def half_kernel(at_ref, own_ref, other_ref, out_ref):
    parity = at_ref[0] % 2
    own_fits = jnp.where(marked(own_ref) >= 5.0, 1, 0) == parity
    other_fits = jnp.where(marked(other_ref) >= 5.0, 1, 0) == parity
    taken = jnp.where(own_fits, own_ref[...], other_ref[...])
    out_ref[0 : EXTRA - 16, :] = taken[0 : EXTRA - 16]
    tail = taken[EXTRA - 16 : EXTRA].astype(jnp.float32)
    clash = (iota(tail.shape, 0) == 15) & (own_fits == other_fits)
    out_ref[EXTRA - 16 : EXTRA, :] = jnp.where(clash, 0.0, tail).astype(jnp.bfloat16)


def block_kernel(at_ref, *refs):
    chunks, extras, out_ref = refs[0:8], refs[8:12], refs[12]
    for slot, chunk_ref in enumerate(chunks):
        out_ref[slot * CHUNK : (slot + 1) * CHUNK, :] = chunk_ref[...]
    wanted = owner_at(at_ref, 0, 0).astype(jnp.float32) + 1.0
    found = jnp.zeros((1, 1), jnp.float32)
    held = jnp.ones((1, 1), jnp.float32)
    taken = extras[0][...]
    for index in range(4):
        mark = marked(extras[index])
        found = found + jnp.where(mark == wanted, 1.0, 0.0)
        held = jnp.where(mark == 0.0, 0.0, held)
        if index > 0:
            taken = jnp.where(mark == wanted, extras[index][...], taken)
    good = jnp.where((found == 1.0) & (held == 1.0), 1.0, 0.0)
    out_ref[MAIN : BLOCK - 16, :] = taken[0 : EXTRA - 16]
    tail = taken[EXTRA - 16 : EXTRA].astype(jnp.float32)
    out_ref[BLOCK - 16 : BLOCK, :] = jnp.where(iota(tail.shape, 0) == 14, good, tail).astype(jnp.bfloat16)


def told_of(ref):
    total = jnp.zeros((16, MAIN), jnp.float32)
    for index in range(1, OWNERS + 1):
        total = total + ref[index * CHUNK - 16 : index * CHUNK, 0:MAIN].astype(jnp.float32)
    end = ref[BLOCK - 16 : BLOCK, 0:128].astype(jnp.float32)
    total = jnp.concatenate([total, end], axis=1)[:, 0:BLOCK]
    return total[10:11], total[11:12] + total[12:13] + total[13:14], end[14:15, 0:1]


def column_of(row):
    count = row.shape[1]
    diagonal = iota((count, count), 0) == iota((count, count), 1)
    return jnp.sum(jnp.where(diagonal, row, 0.0), axis=1, keepdims=True)


def match_kernel(left_count, right_count, own, checked, *refs):
    blocks, out_refs = refs[: left_count + right_count], refs[left_count + right_count :]
    told = [told_of(ref) for ref in blocks]
    best = [jnp.full((1, BLOCK), LOW, jnp.float32)] * left_count
    for right in range(left_count, left_count + right_count):
        ids, inverse = column_of(told[right][0]), column_of(told[right][1])
        rows = blocks[right][...]
        for left in range(left_count):
            scores = dot_nt(rows, blocks[left][...]) * inverse
            alike = ids == told[left][0]
            if own and left == 0 and right == left_count:
                alike = alike & (iota(scores.shape, 0) != iota(scores.shape, 1))
            best[left] = jnp.maximum(best[left], jnp.max(jnp.where(alike, scores, LOW), axis=0, keepdims=True))
    for left in range(left_count):
        out_refs[left][...] = jnp.full(out_refs[left].shape, -1.0, jnp.float32)
        out_refs[left][0:1, 0:BLOCK] = jnp.maximum(best[left] * told[left][1], -1.0)
    if checked:
        good = jnp.minimum(told[0][2], told[left_count][2])
        out_refs[0][1:2, :] = jnp.broadcast_to(good, (1, LANES))


def far_kernel(upper_ref, lower_ref, *refs):
    rights, out_ref, left = refs[0:4], refs[4], refs[5]
    left[0 : BLOCK // 2, :] = upper_ref[...]
    left[BLOCK // 2 : BLOCK, :] = lower_ref[...]
    match_kernel(1, 4, False, False, left, *rights, out_ref)


def final_kernel(at_ref, own_ref, side_ref, z1_ref, z2_ref, z3_ref, known_ref, out_ref, ok_ref):
    sources = {1: z1_ref, 2: z2_ref, 3: z3_ref}
    vectors, groups, good = [], [], jnp.ones((1, LANES), jnp.float32)
    for dx, dz in ((0, 0), *STEPS):
        ref, row = (side_ref if dx else own_ref, 0) if dz == 0 else (sources[dz], 8 * dx)
        vectors.append(ref[row : row + 1, :])
        groups.append(owner_at(at_ref, dx, dz).astype(jnp.float32))
        good = jnp.minimum(good, ref[row + 1 : row + 2, :])
    parts = three_parts(jnp.concatenate(vectors, axis=0))
    pick = as_bf16(iota((LANES, ROWS), 0) == known_ref[0:1, :].astype(jnp.int32))
    picked = dot_nn(jnp.concatenate(parts, axis=0).astype(jnp.bfloat16), pick)
    picked = picked[0:8] + picked[8:16] + picked[16:24]
    total = jnp.zeros((1, ROWS), jnp.float32)
    for index, group in enumerate(groups):
        total = jnp.where(known_ref[1:2, :] == group, picked[index : index + 1], total)
    out_ref[...] = total.reshape(ROWS)
    ok_ref[...] = jnp.where(good[:, 0:128] == 1.0, 1, 0)


SMEM = pl.BlockSpec(memory_space=pltpu.SMEM)


def call(kernel, outs, *args, scalars=0, scratch=(), flops=0):
    read = sum(math.prod(a.shape) * a.dtype.itemsize for a in args)
    return pl.pallas_call(
        kernel,
        out_shape=outs,
        in_specs=[SMEM] * scalars + [VMEM] * (len(args) - scalars),
        out_specs=[VMEM] * len(outs) if isinstance(outs, list) else VMEM,
        scratch_shapes=list(scratch),
        compiler_params=PARAMS,
        cost_estimate=pl.CostEstimate(flops=flops, bytes_accessed=read, transcendentals=0),
    )(*args)


def along_sub(value, to_x, to_z):
    perm = [(4 * x + z, 4 * to_x(x) + to_z(z)) for x in range(4) for z in range(4)]
    return lax.ppermute(value, "sub", perm)


def along_grp(value, to_y, to_core):
    perm = [(2 * y + c, 2 * to_y(y) + to_core(c)) for y in range(4) for c in range(2)]
    return lax.ppermute(value, "grp", perm)


def after(value, other):
    return lax.optimization_barrier((value, other))[0]


def same(index):
    return index


def shift(amount):
    return lambda index: (index + amount) % 4


def flip(amount):
    return lambda index: index ^ amount


def local(embeddings, cluster_ids):
    f32, bf16 = jnp.float32, jnp.bfloat16
    width = embeddings.shape[1]
    shape = jax.ShapeDtypeStruct
    sub = lax.axis_index("sub")
    at = jnp.stack([sub // 4, sub % 4]).astype(jnp.int32)
    *chunks, extra, known = call(
        sort_kernel,
        [shape((CHUNK, width), bf16)] * OWNERS + [shape((EXTRA, width), bf16), shape((8, ROWS), f32)],
        at,
        cluster_ids,
        embeddings,
        scalars=1,
        flops=500_000_000,
    )
    other_extra = along_sub(extra, flip(1), same)
    got = [chunks[0]]
    for slot, (dx, dz) in enumerate(STEPS, 1):
        chunk = chunks[slot]
        if slot > 3:
            chunk = after(chunk, other_extra if slot == 4 else got[slot - 4])
        got.append(along_sub(chunk, flip(dx), shift(dz)))
    extra = call(half_kernel, shape((EXTRA, width), bf16), at, extra, other_extra, scalars=1)
    extras = [extra] + [along_sub(extra, same, shift(dz)) for dz in (1, 2, 3)]
    block = call(block_kernel, shape((BLOCK, width), bf16), at, *got, *extras, scalars=1)
    half = BLOCK // 2
    below = along_grp(block, shift(1), same)
    above = along_grp(block, shift(-1), same)
    across = along_sub(block, shift(2), same)
    sibling = along_grp(block, same, flip(1))
    far = (along_grp(below[:half], shift(1), same), along_grp(above[half:], shift(-1), same))
    across_sibling = along_grp(across, same, flip(1))

    flops = 2 * BLOCK * BLOCK * width
    vector = shape((8, LANES), f32)

    def match(lefts, rights, own=False, checked=False):
        counts = len(lefts), len(rights)
        kernel = functools.partial(match_kernel, *counts, own, checked)
        return call(kernel, [vector] * counts[0], *lefts, *rights, flops=flops * counts[0] * counts[1])

    near, others = (block, sibling), (across, across_sibling)
    best_near, below_near, above_near = match((block, below, above), near, own=True)
    best, below_other, above_other = match((block, below, above), others, checked=True)
    from_above = along_grp(jnp.maximum(below_near, below_other), shift(-1), same)
    from_below = along_grp(jnp.maximum(above_near, above_other), shift(1), same)
    best_far = call(
        far_kernel,
        vector,
        *far,
        *near,
        *others,
        scratch=[pltpu.VMEM((BLOCK, width), bf16)],
        flops=4 * flops,
    )
    from_far = along_grp(best_far, shift(2), same)
    best = jnp.maximum(jnp.maximum(best, best_near), jnp.maximum(from_above, from_below))
    best = jnp.maximum(best, from_far)
    side = along_sub(best, flip(1), same)
    both = jnp.concatenate([best, side], axis=0)
    pulled = [along_sub(both, same, shift(-dz)) for dz in (1, 2, 3)]
    out, ok = call(
        final_kernel,
        [shape((ROWS,), f32), shape((1, 128), jnp.int32)],
        at,
        best,
        side,
        *pulled,
        known,
        scalars=1,
    )
    return lax.cond(ok[0, 0] == 1, lambda e, c, o: o, lambda e, c, o: general(e, c), embeddings, cluster_ids, out)


def solution(mesh):
    return jax.shard_map(
        local,
        mesh=mesh,
        in_specs=(P(("grp", "sub"), None), P(("grp", "sub"))),
        out_specs=P(("grp", "sub")),
        check_vma=False,
    )
```

```python
import functools
import math

import jax
import jax.numpy as jnp
from jax import lax
from jax.experimental import pallas as pl
from jax.experimental.pallas import tpu as pltpu
from jax.sharding import PartitionSpec as P

KG = 3
CAP = 96
EPSILON = 1e-06

ROWS = 384
OWNERS = 8
CHUNK = 48
LIGHT = 42
MAIN = OWNERS * CHUNK
EXTRA = 64
LANES = 512
BLOCK = 352
UPPER = BLOCK // 2
EXTRA_LANE = 384
LOW = -1e30

STEPS = ((0, 0), (1, 1), (1, 3), (1, 2), (0, 2), (0, 1), (0, 3), (1, 0))

VMEM = pl.BlockSpec(memory_space=pltpu.VMEM)
PARAMS = pltpu.CompilerParams(vmem_limit_bytes=48 * 1024 * 1024)


def inverse_norms(block):
    values = block.astype(jnp.float32)
    return lax.rsqrt(jnp.sum(values * values, axis=1) + EPSILON)


def tile_max(left_rows, left_ids, left_inverse, right_rows, right_ids, right_inverse, left_first, right_first):
    scores = lax.dot_general(
        left_rows, right_rows, (((1,), (1,)), ((), ())), preferred_element_type=jnp.float32
    )
    scaled = scores * left_inverse[:, None] * right_inverse[None, :]
    left_index = left_first + jnp.arange(left_rows.shape[0], dtype=jnp.int32)
    right_index = right_first + jnp.arange(right_rows.shape[0], dtype=jnp.int32)
    same_cluster = (
        (left_ids[:, None] == right_ids[None, :])
        & (left_ids[:, None] >= 0)
        & (left_index[:, None] != right_index[None, :])
    )
    masked = jnp.where(same_cluster, scaled, jnp.float32(-1.0))
    return jnp.max(masked, axis=1)


def general(embeddings, cluster_ids):
    groups_count = lax.axis_size("grp")
    feature_count = embeddings.shape[1]
    destination = cluster_ids // KG
    onehot = (destination[:, None] == jnp.arange(groups_count, dtype=jnp.int32)[None, :]).astype(jnp.int32)
    earlier = jnp.cumsum(onehot, axis=0) - onehot
    slot_index = jnp.sum(earlier * onehot, axis=1)
    position = destination * CAP + slot_index
    send_rows = jnp.zeros((groups_count * CAP, feature_count), jnp.bfloat16).at[position].set(embeddings)
    send_ids = (
        jnp.full((groups_count * CAP,), -1.0, jnp.bfloat16).at[position].set(cluster_ids.astype(jnp.bfloat16))
    )
    own_rows = lax.all_to_all(send_rows, "grp", split_axis=0, concat_axis=0, tiled=True)
    own_ids = lax.all_to_all(send_ids, "grp", split_axis=0, concat_axis=0, tiled=True)
    own_count = own_rows.shape[0]
    own_inverse = inverse_norms(own_rows)
    sub_count = lax.axis_size("sub")
    own_sub = lax.axis_index("sub")
    ring = [(index, (index + 1) % sub_count) for index in range(sub_count)]

    def one_block(index, state):
        right_rows, right_ids, current = state
        row_max = tile_max(
            own_rows,
            own_ids,
            own_inverse,
            right_rows,
            right_ids,
            inverse_norms(right_rows),
            own_sub * own_count,
            ((own_sub - index) % sub_count) * own_count,
        )
        next_rows = lax.ppermute(right_rows, "sub", ring)
        next_ids = lax.ppermute(right_ids, "sub", ring)
        return next_rows, next_ids, jnp.maximum(current, row_max)

    start = (own_rows, own_ids, jnp.full((own_count,), -1.0, jnp.float32))
    best_seen = lax.fori_loop(0, sub_count, one_block, start)[2]
    gathered_back = lax.all_to_all(best_seen, "grp", split_axis=0, concat_axis=0, tiled=True)
    return jnp.take(gathered_back, position, axis=0)


def iota(shape, dim):
    return lax.broadcasted_iota(jnp.int32, shape, dim)


def dot_nt(left, right):
    return lax.dot_general(left, right, (((1,), (1,)), ((), ())), preferred_element_type=jnp.float32)


def dot_nn(left, right):
    return lax.dot_general(left, right, (((1,), (0,)), ((), ())), preferred_element_type=jnp.float32)


def three_parts(value):
    high = value.astype(jnp.bfloat16).astype(jnp.float32)
    rest = value - high
    middle = rest.astype(jnp.bfloat16).astype(jnp.float32)
    low = (rest - middle).astype(jnp.bfloat16).astype(jnp.float32)
    return high, middle, low


def as_bf16(mask):
    return jnp.where(mask, 1.0, 0.0).astype(jnp.bfloat16)


def owner_at(place_ref, dx, dz):
    return ((place_ref[0] + dx) % 2) * 4 + (place_ref[1] + dz) % 4


def sort_kernel(at_ref, ids_ref, rows_ref, *out_refs):
    chunk_refs, extra_ref, known_ref = out_refs[:OWNERS], out_refs[OWNERS], out_refs[OWNERS + 1]
    ids = ids_ref[...].reshape(1, ROWS)
    group_of = iota((OWNERS, ROWS), 0)
    member = (ids >= group_of * KG) & (ids < group_of * KG + KG)
    member_f = jnp.where(member, 1.0, 0.0)
    before = as_bf16(iota((ROWS, ROWS), 0) < iota((ROWS, ROWS), 1))
    ranks = dot_nn(member_f.astype(jnp.bfloat16), before)
    rank = jnp.sum(member_f * ranks, axis=0, keepdims=True)
    group = jnp.sum(member_f * group_of.astype(jnp.float32), axis=0, keepdims=True)
    count = jnp.sum(member_f, axis=1, keepdims=True)
    most = jnp.where(count > 64.0, 1.0, 0.0)
    home = jnp.sum(most * iota((OWNERS, 1), 0).astype(jnp.float32), axis=0, keepdims=True)
    values = rows_ref[...].astype(jnp.float32)
    inverse_column = lax.rsqrt(jnp.sum(values * values, axis=1, keepdims=True) + EPSILON)
    diagonal = iota((ROWS, ROWS), 0) == iota((ROWS, ROWS), 1)
    inverse = jnp.sum(jnp.where(diagonal, inverse_column, 0.0), axis=0, keepdims=True)
    high, middle, low = three_parts(inverse)
    line = iota((16, ROWS), 0)
    told = jnp.where(line == 10, ids.astype(jnp.float32) + 1.0, 0.0)
    told = jnp.where(line == 11, high, told)
    told = jnp.where(line == 12, middle, told)
    told = jnp.where(line == 13, low, told)
    rest = (group == home) & (rank >= float(LIGHT))
    place = jnp.where(rest, rank + float(MAIN - LIGHT), -1.0)
    lane = jnp.where(rest, rank + float(EXTRA_LANE - LIGHT), -1.0)
    tolds = []
    for slot, (dx, dz) in enumerate(STEPS):
        goes = (group == owner_at(at_ref, dx, dz).astype(jnp.float32)) & (rank < float(LIGHT))
        place = jnp.where(goes, rank + float(slot * CHUNK), place)
        lane = jnp.where(goes, rank + float(slot * LIGHT), lane)
        tolds.append(jnp.where(goes, told, 0.0))
    tolds.append(jnp.where(rest, told, 0.0))
    known_ref[...] = jnp.where(line == 0, lane, group)[0:8]
    pick = as_bf16(iota((LANES, ROWS), 0) == place.astype(jnp.int32))
    data = dot_nn(pick, rows_ref[...])
    placed = dot_nt(jnp.concatenate(tolds, axis=0).astype(jnp.bfloat16), pick)
    for slot, ref in enumerate(chunk_refs):
        first = slot * CHUNK
        ref[0:32, :] = data[first : first + 32].astype(jnp.bfloat16)
        tail = data[first + 32 : first + CHUNK]
        ref[32:CHUNK, :] = tail.astype(jnp.bfloat16)
        ref[32:CHUNK, 0:LANES] = (tail[:, 0:LANES] + placed[16 * slot : 16 * slot + 16]).astype(jnp.bfloat16)
    extra_ref[0:48, :] = data[MAIN : MAIN + 48].astype(jnp.bfloat16)
    tail = data[MAIN + 48 : MAIN + EXTRA]
    tail = jnp.where(iota(tail.shape, 0) == 15, home + 1.0, tail)
    extra_ref[48:EXTRA, :] = tail.astype(jnp.bfloat16)
    extra_ref[48:EXTRA, 0:128] = (
        tail[:, 0:128] + placed[16 * OWNERS : 16 * OWNERS + 16, MAIN:LANES]
    ).astype(jnp.bfloat16)


def marked(ref):
    return ref[EXTRA - 16 : EXTRA, :].astype(jnp.float32)[15:16, 0:1]


def half_kernel(at_ref, own_ref, other_ref, out_ref):
    parity = at_ref[0] % 2
    own_fits = jnp.where(marked(own_ref) >= 5.0, 1, 0) == parity
    other_fits = jnp.where(marked(other_ref) >= 5.0, 1, 0) == parity
    taken = jnp.where(own_fits, own_ref[...], other_ref[...])
    out_ref[0 : EXTRA - 16, :] = taken[0 : EXTRA - 16]
    tail = taken[EXTRA - 16 : EXTRA].astype(jnp.float32)
    clash = (iota(tail.shape, 0) == 15) & (own_fits == other_fits)
    out_ref[EXTRA - 16 : EXTRA, :] = jnp.where(clash, 0.0, tail).astype(jnp.bfloat16)


def extra_kernel(at_ref, *refs):
    extras, out_ref = refs[0:4], refs[4]
    wanted = owner_at(at_ref, 0, 0).astype(jnp.float32) + 1.0
    found = jnp.zeros((1, 1), jnp.float32)
    held = jnp.ones((1, 1), jnp.float32)
    taken = extras[0][...]
    for index in range(4):
        mark = marked(extras[index])
        found = found + jnp.where(mark == wanted, 1.0, 0.0)
        held = jnp.where(mark == 0.0, 0.0, held)
        if index > 0:
            taken = jnp.where(mark == wanted, extras[index][...], taken)
    good = jnp.where((found == 1.0) & (held == 1.0), 1.0, 0.0)
    out_ref[0 : EXTRA - 16, :] = taken[0 : EXTRA - 16]
    tail = taken[EXTRA - 16 : EXTRA].astype(jnp.float32)
    out_ref[EXTRA - 16 : EXTRA, :] = jnp.where(iota(tail.shape, 0) == 14, good, tail).astype(jnp.bfloat16)


def block_kernel(*refs):
    chunk_refs, out_ref, whole = refs[0:8], refs[8], refs[9]
    total = jnp.zeros((16, MAIN), jnp.float32)
    for slot, chunk_ref in enumerate(chunk_refs):
        whole[slot * CHUNK : (slot + 1) * CHUNK, :] = chunk_ref[...]
        total = total + chunk_ref[CHUNK - 16 : CHUNK, 0:MAIN].astype(jnp.float32)
    row = iota((BLOCK, MAIN), 0)
    source = row
    for slot in range(1, OWNERS):
        source = source + jnp.where(row >= slot * LIGHT, CHUNK - LIGHT, 0)
    source = jnp.where(row < OWNERS * LIGHT, source, -1)
    pick = as_bf16(iota((BLOCK, MAIN), 1) == source)
    data = dot_nn(pick, whole[...])
    told = dot_nt(total.astype(jnp.bfloat16), pick)
    line = iota((16, BLOCK), 0)
    told = jnp.where((line >= 10) & (line <= 13), told, 0.0)
    out_ref[0 : BLOCK - 16, :] = data[0 : BLOCK - 16].astype(jnp.bfloat16)
    out_ref[BLOCK - 16 : BLOCK, :] = jnp.zeros((16, out_ref.shape[1]), jnp.bfloat16)
    out_ref[BLOCK - 16 : BLOCK, 0:BLOCK] = told.astype(jnp.bfloat16)


def told_of(ref):
    count = ref.shape[0]
    end = ref[count - 16 : count, 0:BLOCK].astype(jnp.float32)[:, 0:count]
    return end[10:11], end[11:12] + end[12:13] + end[13:14]


def column_of(row):
    count = row.shape[1]
    diagonal = iota((count, count), 0) == iota((count, count), 1)
    return jnp.sum(jnp.where(diagonal, row, 0.0), axis=1, keepdims=True)


def best_over(lefts, rights, shared):
    best = [jnp.full((1, left.shape[0]), LOW, jnp.float32) for left, _ in lefts]
    for right_index, (right, (right_ids, right_inverse)) in enumerate(rights):
        ids, inverse = column_of(right_ids), column_of(right_inverse)
        rows = right[...]
        for left_index, (left, (left_ids, _)) in enumerate(lefts):
            scores = dot_nt(rows, left[...]) * inverse
            alike = ids == left_ids
            if shared and left_index == 0 and right_index == 0:
                row, column = iota(scores.shape, 0), iota(scores.shape, 1)
                alike = alike & ((row != column) | (row >= shared))
            top = jnp.max(jnp.where(alike, scores, LOW), axis=0, keepdims=True)
            best[left_index] = jnp.maximum(best[left_index], top)
    return best


def scaled(best, inverse):
    return jnp.maximum(best * inverse, -1.0)


def main_kernel(left_count, own, *refs):
    out_refs = refs[len(refs) - left_count :]
    blocks = [(ref, told_of(ref)) for ref in refs[: len(refs) - left_count]]
    lefts = blocks[:left_count]
    best = best_over(lefts, blocks[left_count:], BLOCK if own else 0)
    for out_ref, (_, (_, inverse)), top in zip(out_refs, lefts, best):
        out_ref[...] = jnp.full(out_ref.shape, -1.0, jnp.float32)
        out_ref[0:1, 0:BLOCK] = scaled(top, inverse)


def stack(refs, whole):
    told = [told_of(ref) for ref in refs]
    for index, ref in enumerate(refs):
        whole[index * EXTRA : (index + 1) * EXTRA, :] = ref[...]
    return whole, tuple(jnp.concatenate([part[index] for part in told], axis=1) for index in range(2))


def extras_kernel(count, *refs):
    blocks, extras, rights, right_extras = (
        refs[:count],
        refs[count : 2 * count],
        refs[2 * count : 2 * count + 4],
        refs[2 * count + 4 : 2 * count + 8],
    )
    out_refs, left_whole, right_whole = refs[2 * count + 8 : -2], refs[-2], refs[-1]
    lefts = [(ref, told_of(ref)) for ref in blocks]
    left_stack, right_stack = stack(extras, left_whole), stack(right_extras, right_whole)
    best = best_over(lefts, [right_stack], 0)
    (extra_best,) = best_over(
        [left_stack], [right_stack, *[(ref, told_of(ref)) for ref in rights]], EXTRA if count > 1 else 0
    )
    extra_best = scaled(extra_best, left_stack[1][1])
    bad = jnp.zeros((1, 1), jnp.float32)
    for ref in right_extras:
        bad = jnp.maximum(bad, 1.0 - ref[EXTRA - 16 : EXTRA, :].astype(jnp.float32)[14:15, 0:1])
    for index, out_ref in enumerate(out_refs):
        out_ref[...] = jnp.full(out_ref.shape, -1.0, jnp.float32)
        out_ref[0:1, 0:BLOCK] = scaled(best[index], lefts[index][1][1])
        out_ref[0:1, EXTRA_LANE : EXTRA_LANE + EXTRA] = extra_best[:, index * EXTRA : (index + 1) * EXTRA]
        out_ref[1:2, :] = jnp.broadcast_to(bad if count > 1 else jnp.zeros_like(bad), (1, LANES))


def far_kernel(upper_ref, lower_ref, *refs):
    rights, out_ref, left = refs[:4], refs[4], refs[5]
    left[0:UPPER, :] = upper_ref[...]
    left[UPPER:BLOCK, :] = lower_ref[...]
    main_kernel(1, False, left, *rights, out_ref)


def far_extras_kernel(upper_ref, lower_ref, *refs):
    left = refs[-3]
    left[0:UPPER, :] = upper_ref[...]
    left[UPPER:BLOCK, :] = lower_ref[...]
    extras_kernel(1, left, *refs[:-3], *refs[-2:])


def final_kernel(at_ref, own_ref, side_ref, z1_ref, z2_ref, z3_ref, known_ref, out_ref, ok_ref):
    sources = {1: z1_ref, 2: z2_ref, 3: z3_ref}
    vectors, groups, bad = [], [], jnp.zeros((1, LANES), jnp.float32)
    for dx, dz in STEPS:
        ref, row = (side_ref if dx else own_ref, 0) if dz == 0 else (sources[dz], 8 * dx)
        vectors.append(ref[row : row + 1, :])
        groups.append(owner_at(at_ref, dx, dz).astype(jnp.float32))
        bad = jnp.maximum(bad, ref[row + 1 : row + 2, :])
    parts = three_parts(jnp.concatenate(vectors, axis=0))
    pick = as_bf16(iota((LANES, ROWS), 0) == known_ref[0:1, :].astype(jnp.int32))
    picked = dot_nn(jnp.concatenate(parts, axis=0).astype(jnp.bfloat16), pick)
    picked = picked[0:8] + picked[8:16] + picked[16:24]
    total = jnp.zeros((1, ROWS), jnp.float32)
    for index, group in enumerate(groups):
        total = jnp.where(known_ref[1:2, :] == group, picked[index : index + 1], total)
    out_ref[...] = total.reshape(ROWS)
    ok_ref[...] = jnp.where(bad[:, 0:128] == 0.0, 1, 0)


SMEM = pl.BlockSpec(memory_space=pltpu.SMEM)


def call(kernel, outs, *args, scalars=0, scratch=(), flops=0):
    read = sum(math.prod(a.shape) * a.dtype.itemsize for a in args)
    return pl.pallas_call(
        kernel,
        out_shape=outs,
        in_specs=[SMEM] * scalars + [VMEM] * (len(args) - scalars),
        out_specs=[VMEM] * len(outs) if isinstance(outs, list) else VMEM,
        scratch_shapes=list(scratch),
        compiler_params=PARAMS,
        cost_estimate=pl.CostEstimate(flops=flops, bytes_accessed=read, transcendentals=0),
    )(*args)


def along(value, move):
    def index(y, core, x, z):
        return ((2 * (y % 4) + core) * 4 + x % 4) * 4 + z % 4

    places = [(y, core, x, z) for y in range(4) for core in range(2) for x in range(4) for z in range(4)]
    return lax.ppermute(value, ("grp", "sub"), [(index(*place), index(*move(*place))) for place in places])


def partner(core, x):
    return x ^ (3 if core else 1)


def to_owner(dx, dz):
    return lambda y, core, x, z: (y, core, partner(core, x) if dx else x, z + dz)


def to_y(amount):
    return lambda y, core, x, z: (y + amount, core, x, z)


def to_sibling(y, core, x, z):
    return y, 1 - core, x, z


def to_across(y, core, x, z):
    return y, core, x + 2, z


def join(value, other):
    return jnp.concatenate([value, other], axis=0)


def after(value, *others):
    return lax.optimization_barrier((value, *others))[0]


def local(embeddings, cluster_ids):
    f32, bf16 = jnp.float32, jnp.bfloat16
    width = embeddings.shape[1]
    shape = jax.ShapeDtypeStruct
    sub = lax.axis_index("sub")
    at = jnp.stack([sub // 4, sub % 4]).astype(jnp.int32)
    *chunks, extra, known = call(
        sort_kernel,
        [shape((CHUNK, width), bf16)] * OWNERS + [shape((EXTRA, width), bf16), shape((8, ROWS), f32)],
        at,
        cluster_ids,
        embeddings,
        scalars=1,
        flops=500_000_000,
    )
    other_extra = along(extra, to_owner(1, 0))
    got = [after(chunks[0], other_extra)]
    got += [along(chunks[slot], to_owner(*STEPS[slot])) for slot in range(1, OWNERS)]
    block = call(
        block_kernel,
        shape((BLOCK, width), bf16),
        *got,
        scratch=[pltpu.VMEM((MAIN, width), bf16)],
    )
    extra = call(half_kernel, shape((EXTRA, width), bf16), at, extra, other_extra, scalars=1)
    extras = [extra] + [along(extra, to_owner(0, dz)) for dz in (1, 3)]
    extras.append(along(after(extra, extras[1]), to_owner(0, 2)))
    extra = call(extra_kernel, shape((EXTRA, width), bf16), at, *extras, scalars=1)
    below = along(block, to_y(1))
    above = along(block, to_y(-1))
    across = along(block, to_across)
    sibling = along(block, to_sibling)
    from_lower = along(join(below[:UPPER], extra), to_y(1))
    from_upper = along(join(above[UPPER:], extra), to_y(-1))
    across_extra = along(after(extra, below, above), to_across)
    from_sibling = along(join(across, extra), to_sibling)
    below_extra, above_extra, sibling_extra = from_lower[UPPER:], from_upper[UPPER:], from_sibling[BLOCK:]
    across_sibling = from_sibling[:BLOCK]
    far, far_extra = (from_lower[:UPPER], from_upper[:UPPER]), along(below_extra, to_y(1))
    vector = shape((8, LANES), f32)
    flops = 2 * BLOCK * BLOCK * width
    blocks, rights = (block, below, above), (block, sibling, across, across_sibling)
    extras = (extra, below_extra, above_extra)
    wholes = [pltpu.VMEM((count * EXTRA, width), bf16) for count in (3, 4)]
    near = call(functools.partial(main_kernel, 3, True), [vector] * 3, *blocks, *rights[:2], flops=6 * flops)
    others = call(functools.partial(main_kernel, 3, False), [vector] * 3, *blocks, *rights[2:], flops=6 * flops)
    across_sibling_extra = along(after(across_extra, near[0], others[0]), to_sibling)
    right_extras = (extra, sibling_extra, across_extra, across_sibling_extra)
    added = call(
        functools.partial(extras_kernel, 3),
        [vector] * 3,
        *blocks,
        *extras,
        *rights,
        *right_extras,
        scratch=wholes,
        flops=5 * flops,
    )
    best, best_below, best_above = [
        jnp.maximum(jnp.maximum(first, second), third) for first, second, third in zip(near, others, added)
    ]
    from_above = along(best_below, to_y(-1))
    from_below = along(best_above, to_y(1))
    left = pltpu.VMEM((BLOCK, width), bf16)
    best_far = call(far_kernel, vector, *far, *rights, scratch=[left], flops=4 * flops)
    added_far = call(
        far_extras_kernel,
        vector,
        *far,
        far_extra,
        *rights,
        *right_extras,
        scratch=[left, pltpu.VMEM((EXTRA, width), bf16), wholes[1]],
        flops=2 * flops,
    )
    from_far = along(jnp.maximum(best_far, added_far), to_y(2))
    best = jnp.maximum(best, jnp.maximum(from_above, from_below))
    best = jnp.maximum(best, from_far)
    side = along(best, to_owner(1, 0))
    both = jnp.concatenate([best, side], axis=0)
    pulled = [along(both, to_owner(0, -dz)) for dz in (1, 2, 3)]
    out, ok = call(
        final_kernel,
        [shape((ROWS,), f32), shape((1, 128), jnp.int32)],
        at,
        best,
        side,
        *pulled,
        known,
        scalars=1,
    )
    return lax.cond(ok[0, 0] == 1, lambda e, c, o: o, lambda e, c, o: general(e, c), embeddings, cluster_ids, out)


def solution(mesh):
    return jax.shard_map(
        local,
        mesh=mesh,
        in_specs=(P(("grp", "sub"), None), P(("grp", "sub"))),
        out_specs=P(("grp", "sub")),
        check_vma=False,
    )
```

```python
import functools
import math

import jax
import jax.numpy as jnp
from jax import lax
from jax.experimental import pallas as pl
from jax.experimental.pallas import tpu as pltpu
from jax.sharding import PartitionSpec as P

KG = 3
CAP = 96
EPSILON = 1e-06

ROWS = 384
OWNERS = 8
CHUNK = 48
LIGHT = 42
MAIN = OWNERS * CHUNK
EXTRA = 64
LANES = 512
BLOCK = 352
UPPER = BLOCK // 2
EXTRA_LANE = 384
LOW = -1e30

STEPS = ((0, 0), (1, 1), (1, 3), (1, 2), (0, 2), (0, 1), (0, 3), (1, 0))

VMEM = pl.BlockSpec(memory_space=pltpu.VMEM)
PARAMS = pltpu.CompilerParams(vmem_limit_bytes=48 * 1024 * 1024)


def inverse_norms(block):
    values = block.astype(jnp.float32)
    return lax.rsqrt(jnp.sum(values * values, axis=1) + EPSILON)


def tile_max(left_rows, left_ids, left_inverse, right_rows, right_ids, right_inverse, left_first, right_first):
    scores = lax.dot_general(
        left_rows, right_rows, (((1,), (1,)), ((), ())), preferred_element_type=jnp.float32
    )
    scaled = scores * left_inverse[:, None] * right_inverse[None, :]
    left_index = left_first + jnp.arange(left_rows.shape[0], dtype=jnp.int32)
    right_index = right_first + jnp.arange(right_rows.shape[0], dtype=jnp.int32)
    same_cluster = (
        (left_ids[:, None] == right_ids[None, :])
        & (left_ids[:, None] >= 0)
        & (left_index[:, None] != right_index[None, :])
    )
    masked = jnp.where(same_cluster, scaled, jnp.float32(-1.0))
    return jnp.max(masked, axis=1)


def general(embeddings, cluster_ids):
    groups_count = lax.axis_size("grp")
    feature_count = embeddings.shape[1]
    destination = cluster_ids // KG
    onehot = (destination[:, None] == jnp.arange(groups_count, dtype=jnp.int32)[None, :]).astype(jnp.int32)
    earlier = jnp.cumsum(onehot, axis=0) - onehot
    slot_index = jnp.sum(earlier * onehot, axis=1)
    position = destination * CAP + slot_index
    send_rows = jnp.zeros((groups_count * CAP, feature_count), jnp.bfloat16).at[position].set(embeddings)
    send_ids = (
        jnp.full((groups_count * CAP,), -1.0, jnp.bfloat16).at[position].set(cluster_ids.astype(jnp.bfloat16))
    )
    own_rows = lax.all_to_all(send_rows, "grp", split_axis=0, concat_axis=0, tiled=True)
    own_ids = lax.all_to_all(send_ids, "grp", split_axis=0, concat_axis=0, tiled=True)
    own_count = own_rows.shape[0]
    own_inverse = inverse_norms(own_rows)
    sub_count = lax.axis_size("sub")
    own_sub = lax.axis_index("sub")
    ring = [(index, (index + 1) % sub_count) for index in range(sub_count)]

    def one_block(index, state):
        right_rows, right_ids, current = state
        row_max = tile_max(
            own_rows,
            own_ids,
            own_inverse,
            right_rows,
            right_ids,
            inverse_norms(right_rows),
            own_sub * own_count,
            ((own_sub - index) % sub_count) * own_count,
        )
        next_rows = lax.ppermute(right_rows, "sub", ring)
        next_ids = lax.ppermute(right_ids, "sub", ring)
        return next_rows, next_ids, jnp.maximum(current, row_max)

    start = (own_rows, own_ids, jnp.full((own_count,), -1.0, jnp.float32))
    best_seen = lax.fori_loop(0, sub_count, one_block, start)[2]
    gathered_back = lax.all_to_all(best_seen, "grp", split_axis=0, concat_axis=0, tiled=True)
    return jnp.take(gathered_back, position, axis=0)


def iota(shape, dim):
    return lax.broadcasted_iota(jnp.int32, shape, dim)


def dot_nt(left, right):
    return lax.dot_general(left, right, (((1,), (1,)), ((), ())), preferred_element_type=jnp.float32)


def dot_nn(left, right):
    return lax.dot_general(left, right, (((1,), (0,)), ((), ())), preferred_element_type=jnp.float32)


def three_parts(value):
    high = value.astype(jnp.bfloat16).astype(jnp.float32)
    rest = value - high
    middle = rest.astype(jnp.bfloat16).astype(jnp.float32)
    low = (rest - middle).astype(jnp.bfloat16).astype(jnp.float32)
    return high, middle, low


def as_bf16(mask):
    return jnp.where(mask, 1.0, 0.0).astype(jnp.bfloat16)


def owner_at(place_ref, dx, dz):
    return ((place_ref[0] + dx) % 2) * 4 + (place_ref[1] + dz) % 4


def sort_kernel(at_ref, ids_ref, rows_ref, *out_refs):
    chunk_refs, extra_ref, known_ref = out_refs[:OWNERS], out_refs[OWNERS], out_refs[OWNERS + 1]
    ids = ids_ref[...].reshape(1, ROWS)
    group_of = iota((OWNERS, ROWS), 0)
    member = (ids >= group_of * KG) & (ids < group_of * KG + KG)
    member_f = jnp.where(member, 1.0, 0.0)
    before = as_bf16(iota((ROWS, ROWS), 0) < iota((ROWS, ROWS), 1))
    ranks = dot_nn(member_f.astype(jnp.bfloat16), before)
    rank = jnp.sum(member_f * ranks, axis=0, keepdims=True)
    group = jnp.sum(member_f * group_of.astype(jnp.float32), axis=0, keepdims=True)
    count = jnp.sum(member_f, axis=1, keepdims=True)
    most = jnp.where(count > 64.0, 1.0, 0.0)
    home = jnp.sum(most * iota((OWNERS, 1), 0).astype(jnp.float32), axis=0, keepdims=True)
    values = rows_ref[...].astype(jnp.float32)
    inverse_column = lax.rsqrt(jnp.sum(values * values, axis=1, keepdims=True) + EPSILON)
    diagonal = iota((ROWS, ROWS), 0) == iota((ROWS, ROWS), 1)
    inverse = jnp.sum(jnp.where(diagonal, inverse_column, 0.0), axis=0, keepdims=True)
    high, middle, low = three_parts(inverse)
    line = iota((16, ROWS), 0)
    told = jnp.where(line == 10, ids.astype(jnp.float32) + 1.0, 0.0)
    told = jnp.where(line == 11, high, told)
    told = jnp.where(line == 12, middle, told)
    told = jnp.where(line == 13, low, told)
    rest = (group == home) & (rank >= float(LIGHT))
    place = jnp.where(rest, rank + float(MAIN - LIGHT), -1.0)
    lane = jnp.where(rest, rank + float(EXTRA_LANE - LIGHT), -1.0)
    tolds = []
    for slot, (dx, dz) in enumerate(STEPS):
        goes = (group == owner_at(at_ref, dx, dz).astype(jnp.float32)) & (rank < float(LIGHT))
        place = jnp.where(goes, rank + float(slot * CHUNK), place)
        lane = jnp.where(goes, rank + float(slot * LIGHT), lane)
        tolds.append(jnp.where(goes, told, 0.0))
    tolds.append(jnp.where(rest, told, 0.0))
    known_ref[...] = jnp.where(line == 0, lane, group)[0:8]
    pick = as_bf16(iota((LANES, ROWS), 0) == place.astype(jnp.int32))
    data = dot_nn(pick, rows_ref[...])
    placed = dot_nt(jnp.concatenate(tolds, axis=0).astype(jnp.bfloat16), pick)
    for slot, ref in enumerate(chunk_refs):
        first = slot * CHUNK
        ref[0:32, :] = data[first : first + 32].astype(jnp.bfloat16)
        tail = data[first + 32 : first + CHUNK]
        ref[32:CHUNK, :] = tail.astype(jnp.bfloat16)
        ref[32:CHUNK, 0:LANES] = (tail[:, 0:LANES] + placed[16 * slot : 16 * slot + 16]).astype(jnp.bfloat16)
    extra_ref[0:48, :] = data[MAIN : MAIN + 48].astype(jnp.bfloat16)
    tail = data[MAIN + 48 : MAIN + EXTRA]
    tail = jnp.where(iota(tail.shape, 0) == 15, home + 1.0, tail)
    extra_ref[48:EXTRA, :] = tail.astype(jnp.bfloat16)
    extra_ref[48:EXTRA, 0:128] = (
        tail[:, 0:128] + placed[16 * OWNERS : 16 * OWNERS + 16, MAIN:LANES]
    ).astype(jnp.bfloat16)


def marked(ref):
    return ref[EXTRA - 16 : EXTRA, :].astype(jnp.float32)[15:16, 0:1]


def half_kernel(at_ref, own_ref, other_ref, out_ref):
    parity = at_ref[0] % 2
    own_fits = jnp.where(marked(own_ref) >= 5.0, 1, 0) == parity
    other_fits = jnp.where(marked(other_ref) >= 5.0, 1, 0) == parity
    taken = jnp.where(own_fits, own_ref[...], other_ref[...])
    out_ref[0 : EXTRA - 16, :] = taken[0 : EXTRA - 16]
    tail = taken[EXTRA - 16 : EXTRA].astype(jnp.float32)
    clash = (iota(tail.shape, 0) == 15) & (own_fits == other_fits)
    out_ref[EXTRA - 16 : EXTRA, :] = jnp.where(clash, 0.0, tail).astype(jnp.bfloat16)


def extra_kernel(at_ref, *refs):
    extras, out_ref = refs[0:4], refs[4]
    wanted = owner_at(at_ref, 0, 0).astype(jnp.float32) + 1.0
    found = jnp.zeros((1, 1), jnp.float32)
    held = jnp.ones((1, 1), jnp.float32)
    taken = extras[0][...]
    for index in range(4):
        mark = marked(extras[index])
        found = found + jnp.where(mark == wanted, 1.0, 0.0)
        held = jnp.where(mark == 0.0, 0.0, held)
        if index > 0:
            taken = jnp.where(mark == wanted, extras[index][...], taken)
    good = jnp.where((found == 1.0) & (held == 1.0), 1.0, 0.0)
    out_ref[0 : EXTRA - 16, :] = taken[0 : EXTRA - 16]
    tail = taken[EXTRA - 16 : EXTRA].astype(jnp.float32)
    out_ref[EXTRA - 16 : EXTRA, :] = jnp.where(iota(tail.shape, 0) == 14, good, tail).astype(jnp.bfloat16)


def block_kernel(*refs):
    chunk_refs, out_ref, whole = refs[0:8], refs[8], refs[9]
    total = jnp.zeros((16, MAIN), jnp.float32)
    for slot, chunk_ref in enumerate(chunk_refs):
        whole[slot * CHUNK : (slot + 1) * CHUNK, :] = chunk_ref[...]
        total = total + chunk_ref[CHUNK - 16 : CHUNK, 0:MAIN].astype(jnp.float32)
    row = iota((BLOCK, MAIN), 0)
    source = row
    for slot in range(1, OWNERS):
        source = source + jnp.where(row >= slot * LIGHT, CHUNK - LIGHT, 0)
    source = jnp.where(row < OWNERS * LIGHT, source, -1)
    pick = as_bf16(iota((BLOCK, MAIN), 1) == source)
    data = dot_nn(pick, whole[...])
    told = dot_nt(total.astype(jnp.bfloat16), pick)
    line = iota((16, BLOCK), 0)
    told = jnp.where((line >= 10) & (line <= 13), told, 0.0)
    out_ref[0 : BLOCK - 16, :] = data[0 : BLOCK - 16].astype(jnp.bfloat16)
    out_ref[BLOCK - 16 : BLOCK, :] = jnp.zeros((16, out_ref.shape[1]), jnp.bfloat16)
    out_ref[BLOCK - 16 : BLOCK, 0:BLOCK] = told.astype(jnp.bfloat16)


def told_of(ref):
    count = ref.shape[0]
    end = ref[count - 16 : count, 0:BLOCK].astype(jnp.float32)[:, 0:count]
    return end[10:11], end[11:12] + end[12:13] + end[13:14]


def column_of(row):
    count = row.shape[1]
    diagonal = iota((count, count), 0) == iota((count, count), 1)
    return jnp.sum(jnp.where(diagonal, row, 0.0), axis=1, keepdims=True)


def best_over(lefts, rights, shared):
    best = [jnp.full((1, left.shape[0]), LOW, jnp.float32) for left, _ in lefts]
    for right_index, (right, (right_ids, right_inverse)) in enumerate(rights):
        ids, inverse = column_of(right_ids), column_of(right_inverse)
        rows = right[...]
        for left_index, (left, (left_ids, _)) in enumerate(lefts):
            scores = dot_nt(rows, left[...]) * inverse
            alike = ids == left_ids
            if shared and left_index == 0 and right_index == 0:
                row, column = iota(scores.shape, 0), iota(scores.shape, 1)
                alike = alike & ((row != column) | (row >= shared))
            top = jnp.max(jnp.where(alike, scores, LOW), axis=0, keepdims=True)
            best[left_index] = jnp.maximum(best[left_index], top)
    return best


def scaled(best, inverse):
    return jnp.maximum(best * inverse, -1.0)


def main_kernel(left_count, own, *refs):
    out_refs = refs[len(refs) - left_count :]
    blocks = [(ref, told_of(ref)) for ref in refs[: len(refs) - left_count]]
    lefts = blocks[:left_count]
    best = best_over(lefts, blocks[left_count:], BLOCK if own else 0)
    for out_ref, (_, (_, inverse)), top in zip(out_refs, lefts, best):
        out_ref[...] = jnp.full(out_ref.shape, -1.0, jnp.float32)
        out_ref[0:1, 0:BLOCK] = scaled(top, inverse)


def stack(refs, whole):
    told = [told_of(ref) for ref in refs]
    for index, ref in enumerate(refs):
        whole[index * EXTRA : (index + 1) * EXTRA, :] = ref[...]
    return whole, tuple(jnp.concatenate([part[index] for part in told], axis=1) for index in range(2))


def extras_kernel(count, *refs):
    blocks, extras, rights, right_extras = (
        refs[:count],
        refs[count : 2 * count],
        refs[2 * count : 2 * count + 4],
        refs[2 * count + 4 : 2 * count + 8],
    )
    out_refs, left_whole, right_whole = refs[2 * count + 8 : -2], refs[-2], refs[-1]
    lefts = [(ref, told_of(ref)) for ref in blocks]
    left_stack, right_stack = stack(extras, left_whole), stack(right_extras, right_whole)
    best = best_over(lefts, [right_stack], 0)
    (extra_best,) = best_over(
        [left_stack], [right_stack, *[(ref, told_of(ref)) for ref in rights]], EXTRA if count > 1 else 0
    )
    extra_best = scaled(extra_best, left_stack[1][1])
    bad = jnp.zeros((1, 1), jnp.float32)
    for ref in right_extras:
        bad = jnp.maximum(bad, 1.0 - ref[EXTRA - 16 : EXTRA, :].astype(jnp.float32)[14:15, 0:1])
    for index, out_ref in enumerate(out_refs):
        out_ref[...] = jnp.full(out_ref.shape, -1.0, jnp.float32)
        out_ref[0:1, 0:BLOCK] = scaled(best[index], lefts[index][1][1])
        out_ref[0:1, EXTRA_LANE : EXTRA_LANE + EXTRA] = extra_best[:, index * EXTRA : (index + 1) * EXTRA]
        out_ref[1:2, :] = jnp.broadcast_to(bad if count > 1 else jnp.zeros_like(bad), (1, LANES))


def far_kernel(upper_ref, lower_ref, *refs):
    rights, out_ref, left = refs[:4], refs[4], refs[5]
    left[0:UPPER, :] = upper_ref[...]
    left[UPPER:BLOCK, :] = lower_ref[...]
    main_kernel(1, False, left, *rights, out_ref)


def far_extras_kernel(upper_ref, lower_ref, *refs):
    left = refs[-3]
    left[0:UPPER, :] = upper_ref[...]
    left[UPPER:BLOCK, :] = lower_ref[...]
    extras_kernel(1, left, *refs[:-3], *refs[-2:])


def final_kernel(at_ref, own_ref, side_ref, z1_ref, z2_ref, z3_ref, known_ref, out_ref, ok_ref):
    sources = {1: z1_ref, 2: z2_ref, 3: z3_ref}
    vectors, groups, bad = [], [], jnp.zeros((1, LANES), jnp.float32)
    for dx, dz in STEPS:
        ref, row = (side_ref if dx else own_ref, 0) if dz == 0 else (sources[dz], 8 * dx)
        vectors.append(ref[row : row + 1, :])
        groups.append(owner_at(at_ref, dx, dz).astype(jnp.float32))
        bad = jnp.maximum(bad, ref[row + 1 : row + 2, :])
    parts = three_parts(jnp.concatenate(vectors, axis=0))
    pick = as_bf16(iota((LANES, ROWS), 0) == known_ref[0:1, :].astype(jnp.int32))
    picked = dot_nn(jnp.concatenate(parts, axis=0).astype(jnp.bfloat16), pick)
    picked = picked[0:8] + picked[8:16] + picked[16:24]
    total = jnp.zeros((1, ROWS), jnp.float32)
    for index, group in enumerate(groups):
        total = jnp.where(known_ref[1:2, :] == group, picked[index : index + 1], total)
    out_ref[...] = total.reshape(ROWS)
    ok_ref[...] = jnp.where(bad[:, 0:128] == 0.0, 1, 0)


SMEM = pl.BlockSpec(memory_space=pltpu.SMEM)


def call(kernel, outs, *args, scalars=0, scratch=(), flops=0):
    read = sum(math.prod(a.shape) * a.dtype.itemsize for a in args)
    return pl.pallas_call(
        kernel,
        out_shape=outs,
        in_specs=[SMEM] * scalars + [VMEM] * (len(args) - scalars),
        out_specs=[VMEM] * len(outs) if isinstance(outs, list) else VMEM,
        scratch_shapes=list(scratch),
        compiler_params=PARAMS,
        cost_estimate=pl.CostEstimate(flops=flops, bytes_accessed=read, transcendentals=0),
    )(*args)


def along(value, move):
    def index(y, core, x, z):
        return ((2 * (y % 4) + core) * 4 + x % 4) * 4 + z % 4

    places = [(y, core, x, z) for y in range(4) for core in range(2) for x in range(4) for z in range(4)]
    return lax.ppermute(value, ("grp", "sub"), [(index(*place), index(*move(*place))) for place in places])


def partner(core, x):
    return x ^ (3 if core else 1)


def to_owner(dx, dz):
    return lambda y, core, x, z: (y, core, partner(core, x) if dx else x, z + dz)


def to_y(amount):
    return lambda y, core, x, z: (y + amount, core, x, z)


def to_sibling(y, core, x, z):
    return y, 1 - core, x, z


def to_across(y, core, x, z):
    return y, core, x + 2, z


def join(value, other):
    return jnp.concatenate([value, other], axis=0)


def after(value, *others):
    return lax.optimization_barrier((value, *others))[0]


def local(embeddings, cluster_ids):
    f32, bf16 = jnp.float32, jnp.bfloat16
    width = embeddings.shape[1]
    shape = jax.ShapeDtypeStruct
    sub = lax.axis_index("sub")
    at = jnp.stack([sub // 4, sub % 4]).astype(jnp.int32)
    *chunks, extra, known = call(
        sort_kernel,
        [shape((CHUNK, width), bf16)] * OWNERS + [shape((EXTRA, width), bf16), shape((8, ROWS), f32)],
        at,
        cluster_ids,
        embeddings,
        scalars=1,
        flops=500_000_000,
    )
    other_extra = along(extra, to_owner(1, 0))
    got = [after(chunks[0], other_extra)]
    got += [along(chunks[slot], to_owner(*STEPS[slot])) for slot in range(1, OWNERS)]
    block = call(
        block_kernel,
        shape((BLOCK, width), bf16),
        *got,
        scratch=[pltpu.VMEM((MAIN, width), bf16)],
    )
    extra = call(half_kernel, shape((EXTRA, width), bf16), at, extra, other_extra, scalars=1)
    extras = [extra] + [along(extra, to_owner(0, dz)) for dz in (1, 3)]
    extras.append(along(after(extra, extras[1]), to_owner(0, 2)))
    extra = call(extra_kernel, shape((EXTRA, width), bf16), at, *extras, scalars=1)
    below = along(block, to_y(1))
    above = along(block, to_y(-1))
    across = along(block, to_across)
    sibling = along(block, to_sibling)
    from_lower = along(join(below[:UPPER], extra), to_y(1))
    from_upper = along(join(above[UPPER:], extra), to_y(-1))
    across_extra = along(after(extra, below, above), to_across)
    from_sibling = along(join(across, extra), to_sibling)
    below_extra, above_extra, sibling_extra = from_lower[UPPER:], from_upper[UPPER:], from_sibling[BLOCK:]
    across_sibling = from_sibling[:BLOCK]
    far, far_extra = (from_lower[:UPPER], from_upper[:UPPER]), along(extra, to_y(2))
    vector = shape((8, LANES), f32)
    flops = 2 * BLOCK * BLOCK * width
    blocks, rights = (block, below, above), (block, sibling, across, across_sibling)
    extras = (extra, below_extra, above_extra)
    wholes = [pltpu.VMEM((count * EXTRA, width), bf16) for count in (3, 4)]
    near = call(functools.partial(main_kernel, 3, True), [vector] * 3, *blocks, *rights[:2], flops=6 * flops)
    others = call(functools.partial(main_kernel, 3, False), [vector] * 3, *blocks, *rights[2:], flops=6 * flops)
    across_sibling_extra = along(after(across_extra, near[0], others[0]), to_sibling)
    right_extras = (extra, sibling_extra, across_extra, across_sibling_extra)
    added = call(
        functools.partial(extras_kernel, 3),
        [vector] * 3,
        *blocks,
        *extras,
        *rights,
        *right_extras,
        scratch=wholes,
        flops=5 * flops,
    )
    best, best_below, best_above = [
        jnp.maximum(jnp.maximum(first, second), third) for first, second, third in zip(near, others, added)
    ]
    from_above = along(best_below, to_y(-1))
    from_below = along(best_above, to_y(1))
    left = pltpu.VMEM((BLOCK, width), bf16)
    best_far = call(far_kernel, vector, *far, *rights, scratch=[left], flops=4 * flops)
    added_far = call(
        far_extras_kernel,
        vector,
        *far,
        far_extra,
        *rights,
        *right_extras,
        scratch=[left, pltpu.VMEM((EXTRA, width), bf16), wholes[1]],
        flops=2 * flops,
    )
    from_far = along(jnp.maximum(best_far, added_far), to_y(2))
    best = jnp.maximum(best, jnp.maximum(from_above, from_below))
    best = jnp.maximum(best, from_far)
    side = along(best, to_owner(1, 0))
    both = jnp.concatenate([best, side], axis=0)
    pulled = [along(both, to_owner(0, -dz)) for dz in (1, 2, 3)]
    out, ok = call(
        final_kernel,
        [shape((ROWS,), f32), shape((1, 128), jnp.int32)],
        at,
        best,
        side,
        *pulled,
        known,
        scalars=1,
    )
    return lax.cond(ok[0, 0] == 1, lambda e, c, o: o, lambda e, c, o: general(e, c), embeddings, cluster_ids, out)


def solution(mesh):
    return jax.shard_map(
        local,
        mesh=mesh,
        in_specs=(P(("grp", "sub"), None), P(("grp", "sub"))),
        out_specs=P(("grp", "sub")),
        check_vma=False,
    )
```
